32 devices in a mesh: gx: 16 (over z, y, x), gy: 2 (over core).
Axes of the slice: x: 2, y: 2, z: 4, core: 2. Of those that a mesh axis runs over, the one named last changes fastest.
Arguments:
- state: float32 [6, 256, 6144], P(None, 'gx', 'gy'), as said below
- shock_height: float32 [256, 32], P('gx'), may hold values from 0.9 to 1.1
- wall_segment: int32 [256], P('gx'), may hold values from 0 to 15, never falling along the last dimension, each value on 1 to 32 neighbouring positions
- segment_level: int32 [16], replicated, may hold values from 0 to 15
- blow_table: float32 [16, 32], replicated, may hold values from 0.1 to 1.5
Outputs:
- state_new: float32 [6, 256, 6144], P(None, 'gx', 'gy')
- shock_new: float32 [256, 32], P('gx')
The draws below stay inside these ranges and needn't reach their ends.
Inputs may be any that keep to these rules, and one draw needn't show every extreme that they name: `state`: each cell has density in [0.5, 2], p / density in [0.6, 2.5], q5 / density in [0.05, 0.6], u in [0, 2], v and w in [-1, 1]. `wall_segment`: segment numbers never fall along the stream; each segment covers 1 to 32 cells.
All inputs are finite; a program needn't handle non-finite values.
Results may differ from the reference program's by a relative error of at most 0.00002.
Values sent between devices are 32-bit elements; how exact they have to be, the bound alone decides.
A program may use at most 64 MiB of HBM per device.

```python
import math
import jax
import jax.numpy as jnp
import numpy as np
from jax import lax

CX = 16
NZ = 32
NLEV = 16
SEG_MOST = 32
NX = 256
NY = 192
NSEG = 16
N_GX = 16


def draw_state(key, part):
    noise_child_seeds = jax.random.split(key, 6)
    processor_arrangement = (NX, NY * NZ)
    specific_volume_inverse = 0.5 * jnp.exp(jax.random.uniform(noise_child_seeds[0], processor_arrangement, jnp.float32, 0.0, math.log(4.0)))
    streamwise_flow_speed = 1.0 + jnp.clip(0.4 * jax.random.normal(noise_child_seeds[1], processor_arrangement, jnp.float32), -1.0, 1.0)
    normal_flow_speed = jnp.clip(0.4 * jax.random.normal(noise_child_seeds[2], processor_arrangement, jnp.float32), -1.0, 1.0)
    crosswise_flow_speed = jnp.clip(0.4 * jax.random.normal(noise_child_seeds[3], processor_arrangement, jnp.float32), -1.0, 1.0)
    heavy_particle_kelvin = 0.6 * jnp.exp(jax.random.uniform(noise_child_seeds[4], processor_arrangement, jnp.float32, 0.0, math.log(2.5 / 0.6)))
    oscillator_share = 0.05 * jnp.exp(jax.random.uniform(noise_child_seeds[5], processor_arrangement, jnp.float32, 0.0, math.log(12.0)))
    stagnation_enthalpy_sum = specific_volume_inverse * heavy_particle_kelvin / 0.4 + 0.5 * specific_volume_inverse * (streamwise_flow_speed * streamwise_flow_speed + normal_flow_speed * normal_flow_speed + crosswise_flow_speed * crosswise_flow_speed) + specific_volume_inverse * oscillator_share
    return jnp.stack([specific_volume_inverse, specific_volume_inverse * streamwise_flow_speed, specific_volume_inverse * normal_flow_speed, specific_volume_inverse * crosswise_flow_speed, stagnation_enthalpy_sum, specific_volume_inverse * oscillator_share]).astype(jnp.float32)


def with_ends(values, own_key, smallest, top_value):
    longest = values.shape.index(max(values.shape))
    spots = []
    for shift in (0, 1):
        where = [jax.random.randint(jax.random.fold_in(own_key, axis), (), 0, length) for axis, length in enumerate(values.shape)]
        where[longest] = (where[longest] + shift) % values.shape[longest]
        spots.append(tuple(where))
    return values.at[spots[0]].set(smallest).at[spots[1]].set(top_value)


def block_scale(own_key, dims, cuts, least, high):
    gain = 1.0
    for dim, blocks in cuts:
        heights = jax.random.uniform(jax.random.fold_in(jax.random.fold_in(own_key, 6), dim), (blocks,), jnp.float32, least / len(cuts), high / len(cuts))
        gain = gain * jnp.repeat(jnp.exp(heights), dims[dim] // blocks).reshape((-1,) + (1,) * (len(dims) - 1 - dim))
    return gain


def split_up(count, total, most, lean):
    portions = [(1 << 20) // math.isqrt(rank ** lean) + 1 for rank in range(2, count + 1)]
    rest, holding = total - most - (count - 1), [1] * (count - 1)
    while rest > 0:
        candidates = [i for i in range(count - 1) if holding[i] < most]
        pool, budget = sum([portions[i] for i in candidates]), rest
        for i in candidates:
            extra = min(most - holding[i], max(1, budget * portions[i] // pool), rest)
            holding[i] = holding[i] + extra
            rest = rest - extra
    return np.array([most] + holding)


def uneven(rng, count, total, reach, lean):
    if count == 2:
        one = jax.random.randint(rng, (), max(1, total - reach), min(reach, total - 1) + 1)
        return jnp.stack([one, total - one])
    tallies = jnp.asarray(split_up(count, total, reach, lean), jnp.int32)
    twos = (count - 1) // 2
    giver, sink = tallies[1:1 + 2 * twos:2], tallies[2:2 + 2 * twos:2]
    room = jnp.minimum(giver - 1, reach - sink)
    moved = jax.random.randint(jax.random.fold_in(rng, 1), (twos,), 0, 1 << 20) % (room + 1)
    tallies = tallies.at[1:1 + 2 * twos:2].set(giver - moved).at[2:2 + 2 * twos:2].set(sink + moved)
    return tallies[jax.random.permutation(jax.random.fold_in(rng, 2), count)]


def setup_inputs(seed: int = 0) -> dict:
    seeds = jax.random.split(jax.random.key(seed), 6)
    state = draw_state(jax.random.fold_in(seeds[5], 71), 0)
    shock_height = jnp.clip(0.9 + 0.20000005 * jax.random.uniform(seeds[1], (NX, NZ), jnp.float32) ** block_scale(seeds[1], (NX, NZ), ((0, 16),), -0.2, 0.2), 0.9, 1.1)
    wall_segment = jnp.searchsorted(jnp.cumsum(uneven(seeds[2], NSEG, NX, SEG_MOST, 0)), jnp.arange(NX), side="right").astype(jnp.int32)
    segment_level = with_ends(jax.random.randint(seeds[3], (NSEG,), 0, NLEV), jax.random.fold_in(seeds[3], 1), 0, NLEV - 1).astype(jnp.int32)
    blow_table = jnp.clip(jax.random.uniform(seeds[4], (NLEV, NZ), jnp.float32, 0.1, 1.5), 0.1, 1.5)
    return dict(state=state, shock_height=shock_height, wall_segment=wall_segment, segment_level=segment_level, blow_table=blow_table)


HEAT_RATIO = 1.4
STREAM_STEP = 0.05
SPAN_STEP = 0.05
STRETCH_RATE = 2.0
CHARACTER_KELVIN = 3.0
WHITE_LAW_FACTOR = 1.0
LANDAU_TELLER = 0.002
FREE_PRESSURE = 0.1
FREE_MACH = 6.0
COURANT = 0.05

def zshift(values, offset, planes):
    length = values.shape[-1]
    plane_at = jnp.arange(length, dtype=jnp.int32) % planes
    if offset > 0:
        return jnp.where(plane_at >= offset, jnp.roll(values, offset, axis=-1), jnp.roll(values, offset - planes, axis=-1))
    return jnp.where(plane_at < planes + offset, jnp.roll(values, offset, axis=-1), jnp.roll(values, offset + planes, axis=-1))

def primitives(conserved):
    specific_volume_inverse = conserved[0]
    vel_x = conserved[1] / specific_volume_inverse
    vel_y = conserved[2] / specific_volume_inverse
    vel_z = conserved[3] / specific_volume_inverse
    thermodynamic_stress = (HEAT_RATIO - 1.0) * (conserved[4] - 0.5 * (conserved[1] * vel_x + conserved[2] * vel_y + conserved[3] * vel_z) - conserved[5])
    sound_speed = jnp.sqrt(HEAT_RATIO * thermodynamic_stress / specific_volume_inverse)
    return (specific_volume_inverse, vel_x, vel_y, vel_z, thermodynamic_stress, sound_speed)

def face_difference(plus_flux, minus_flux, cells, axis_at, stride):

    def window(values, offset):
        return lax.slice_in_dim(values, offset * stride, (offset + cells + 1) * stride, axis=axis_at)
    upwind = (2.0 * window(plus_flux, 0) - 13.0 * window(plus_flux, 1) + 47.0 * window(plus_flux, 2) + 27.0 * window(plus_flux, 3) - 3.0 * window(plus_flux, 4)) / 60.0
    downwind = (-3.0 * window(minus_flux, 1) + 27.0 * window(minus_flux, 2) + 47.0 * window(minus_flux, 3) - 13.0 * window(minus_flux, 4) + 2.0 * window(minus_flux, 5)) / 60.0
    face_sum = upwind + downwind
    return lax.slice_in_dim(face_sum, stride, (cells + 1) * stride, axis=axis_at) - lax.slice_in_dim(face_sum, 0, cells * stride, axis=axis_at)

def stretch(index_rows, total_rows):
    growth = jnp.exp(STRETCH_RATE * (index_rows + 0.5) / total_rows)
    denominator = math.exp(STRETCH_RATE) - 1.0
    return ((growth - 1.0) / denominator, STRETCH_RATE * growth / (total_rows * denominator))

def split_pair(fluxes, speeds, conserved):
    return (0.5 * (fluxes + speeds * conserved), 0.5 * (fluxes - speeds * conserved))

def stream_part(conserved_x, height_ext, spacing_rows, planes):
    columns = conserved_x.shape[1] - 6
    specific_volume_inverse, vel_x, vel_y, vel_z, thermodynamic_stress, sound_speed = primitives(conserved_x)
    metric = SPAN_STEP * jnp.tile(height_ext, (1, conserved_x.shape[2] // planes)) * spacing_rows[None, :]
    fluxes = jnp.stack([conserved_x[1], conserved_x[1] * vel_x + thermodynamic_stress, conserved_x[2] * vel_x, conserved_x[3] * vel_x, (conserved_x[4] + thermodynamic_stress) * vel_x, conserved_x[5] * vel_x]) * metric
    speeds = (jnp.abs(vel_x) + sound_speed) * metric
    plus_flux, minus_flux = split_pair(fluxes, speeds, conserved_x)
    return face_difference(plus_flux, minus_flux, columns, 1, 1)

def normal_part(conserved_y, slope_x, slope_z, shock_rate, eta_rows, planes):
    copies = conserved_y.shape[2] // planes
    row_count = copies - 6
    specific_volume_inverse, vel_x, vel_y, vel_z, thermodynamic_stress, sound_speed = primitives(conserved_y)
    face_area = STREAM_STEP * SPAN_STEP
    metric_x = -face_area * eta_rows[None, :] * jnp.tile(slope_x, (1, copies))
    metric_z = -face_area * eta_rows[None, :] * jnp.tile(slope_z, (1, copies))
    metric_t = -face_area * eta_rows[None, :] * jnp.tile(shock_rate, (1, copies))
    contra = metric_t + metric_x * vel_x + face_area * vel_y + metric_z * vel_z
    fluxes = jnp.stack([conserved_y[0] * contra, conserved_y[1] * contra + metric_x * thermodynamic_stress, conserved_y[2] * contra + face_area * thermodynamic_stress, conserved_y[3] * contra + metric_z * thermodynamic_stress, (conserved_y[4] + thermodynamic_stress) * contra - metric_t * thermodynamic_stress, conserved_y[5] * contra])
    speeds = jnp.abs(contra) + sound_speed * jnp.sqrt(metric_x * metric_x + face_area * face_area + metric_z * metric_z)
    plus_flux, minus_flux = split_pair(fluxes, speeds, conserved_y)
    return face_difference(plus_flux, minus_flux, row_count, 2, planes)

def span_part(conserved, height, spacing_rows, planes):
    specific_volume_inverse, vel_x, vel_y, vel_z, thermodynamic_stress, sound_speed = primitives(conserved)
    metric = STREAM_STEP * jnp.tile(height, (1, conserved.shape[2] // planes)) * spacing_rows[None, :]
    fluxes = jnp.stack([conserved[3], conserved[1] * vel_z, conserved[2] * vel_z, conserved[3] * vel_z + thermodynamic_stress, (conserved[4] + thermodynamic_stress) * vel_z, conserved[5] * vel_z]) * metric
    speeds = (jnp.abs(vel_z) + sound_speed) * metric
    plus_flux, minus_flux = split_pair(fluxes, speeds, conserved)
    upwind = (2.0 * zshift(plus_flux, 2, planes) - 13.0 * zshift(plus_flux, 1, planes) + 47.0 * plus_flux + 27.0 * zshift(plus_flux, -1, planes) - 3.0 * zshift(plus_flux, -2, planes)) / 60.0
    downwind = (-3.0 * zshift(minus_flux, 1, planes) + 27.0 * minus_flux + 47.0 * zshift(minus_flux, -1, planes) - 13.0 * zshift(minus_flux, -2, planes) + 2.0 * zshift(minus_flux, -3, planes)) / 60.0
    face_sum = upwind + downwind
    return face_sum - zshift(face_sum, 1, planes)

def relaxation(conserved):
    specific_volume_inverse, vel_x, vel_y, vel_z, thermodynamic_stress, sound_speed = primitives(conserved)
    heavy_particle_kelvin = thermodynamic_stress / specific_volume_inverse
    oscillator_balanced_share = CHARACTER_KELVIN / (jnp.exp(CHARACTER_KELVIN / heavy_particle_kelvin) - 1.0)
    landau_teller_source = thermodynamic_stress / (LANDAU_TELLER * jnp.exp(WHITE_LAW_FACTOR * jnp.exp(-jnp.log(heavy_particle_kelvin) / 3.0)))
    return specific_volume_inverse * (oscillator_balanced_share - conserved[5] / specific_volume_inverse) * landau_teller_source

def slopes(height_ext, planes):
    columns = height_ext.shape[0] - 6
    slope_x = (height_ext[1:columns + 1] - 8.0 * height_ext[2:columns + 2] + 8.0 * height_ext[4:columns + 4] - height_ext[5:columns + 5]) / (12.0 * STREAM_STEP)
    height = height_ext[3:columns + 3]
    slope_z = (zshift(height, 2, planes) - 8.0 * zshift(height, 1, planes) + 8.0 * zshift(height, -1, planes) - zshift(height, -2, planes)) / (12.0 * SPAN_STEP)
    return (slope_x, slope_z)

def shock_speed(top_row, slope_x, slope_z):
    specific_volume_inverse, vel_x, vel_y, vel_z, thermodynamic_stress, sound_speed = primitives(top_row)
    tilt_norm = jnp.sqrt(1.0 + slope_x * slope_x + slope_z * slope_z)
    normal = (vel_y - vel_x * slope_x - vel_z * slope_z) / tilt_norm
    sine_sq = slope_x * slope_x / (tilt_norm * tilt_norm)
    jump_pressure = FREE_PRESSURE * (1.0 + 2.0 * HEAT_RATIO / (HEAT_RATIO + 1.0) * (FREE_MACH * FREE_MACH * sine_sq - 1.0))
    return tilt_norm * (normal + (jump_pressure - thermodynamic_stress) / (specific_volume_inverse * sound_speed))

def wall_ghosts(first_rows, blowing, planes):
    mirror = jnp.concatenate([first_rows[..., 2 * planes:3 * planes], first_rows[..., planes:2 * planes], first_rows[..., 0:planes]], axis=-1)
    blown_y = 2.0 * jnp.tile(blowing, (1, 3)) - mirror[2]
    stagnation_enthalpy_sum = mirror[4] + 0.5 * (blown_y * blown_y - mirror[2] * mirror[2]) / mirror[0]
    return jnp.stack([mirror[0], mirror[1], blown_y, mirror[3], stagnation_enthalpy_sum, mirror[5]])

def advance(conserved, conserved_x, conserved_y, height_ext, slope_x, slope_z, shock_rate, first_row, total_rows, planes):
    columns = conserved.shape[1]
    row_count = conserved.shape[2] // planes
    local_rows = (first_row + jnp.arange(row_count, dtype=jnp.int32)).astype(jnp.float32)
    eta_local, spacing_local = stretch(local_rows, total_rows)
    spacing_rows = jnp.repeat(spacing_local, planes)
    outer_rows = (first_row - 3 + jnp.arange(row_count + 6, dtype=jnp.int32)).astype(jnp.float32)
    eta_outer = stretch(outer_rows, total_rows)[0]
    eta_rows = jnp.repeat(eta_outer, planes)
    height = height_ext[3:columns + 3]
    divergence = stream_part(conserved_x, height_ext, spacing_rows, planes) + normal_part(conserved_y, slope_x, slope_z, shock_rate, eta_rows, planes) + span_part(conserved, height, spacing_rows, planes)
    height_rows = jnp.tile(height, (1, row_count))
    rate_rows = jnp.tile(shock_rate, (1, row_count))
    volume = STREAM_STEP * SPAN_STEP * height_rows * spacing_rows[None, :]
    change = -divergence / volume - conserved * (rate_rows / height_rows)
    change = jnp.concatenate([change[:5], (change[5] + relaxation(conserved))[None]], axis=0)
    return conserved + COURANT / total_rows * change

def reference(state, shock_height, wall_segment, segment_level, blow_table):
    planes = NZ
    length = NY * NZ
    height_ext = jnp.pad(shock_height, ((3, 3), (0, 0)), mode='edge')
    slope_x, slope_z = slopes(height_ext, planes)
    shock_rate = shock_speed(state[:, :, length - planes:], slope_x, slope_z)
    shock_new = shock_height + COURANT / NY * shock_rate
    blowing = blow_table[segment_level[wall_segment]]
    padded = jnp.pad(state, ((0, 0), (3, 3), (0, 0)), mode='edge')
    zero_idx = jnp.zeros((), jnp.int32)

    def block_step(block_at, result):
        start_col = (block_at * CX).astype(jnp.int32)
        conserved_x = lax.dynamic_slice(padded, (zero_idx, start_col, zero_idx), (6, CX + 6, length))
        conserved = conserved_x[:, 3:CX + 3]
        ext_height = lax.dynamic_slice(height_ext, (start_col, zero_idx), (CX + 6, planes))
        block_sx = lax.dynamic_slice(slope_x, (start_col, zero_idx), (CX, planes))
        block_sz = lax.dynamic_slice(slope_z, (start_col, zero_idx), (CX, planes))
        block_rate = lax.dynamic_slice(shock_rate, (start_col, zero_idx), (CX, planes))
        block_blow = lax.dynamic_slice(blowing, (start_col, zero_idx), (CX, planes))
        conserved_y = jnp.concatenate([wall_ghosts(conserved[..., :3 * planes], block_blow, planes), conserved, jnp.tile(conserved[..., length - planes:], (1, 1, 3))], axis=2)
        updated = advance(conserved, conserved_x, conserved_y, ext_height, block_sx, block_sz, block_rate, 0, NY, planes)
        return lax.dynamic_update_slice(result, updated, (zero_idx, start_col, zero_idx))
    state_new = lax.fori_loop(0, N_GX, block_step, jnp.zeros_like(state))
    return (state_new, shock_new)
```

```python
import functools
import math

import jax
import jax.numpy as jnp
import numpy as np
from jax import lax
from jax.experimental import pallas as pl
from jax.experimental.pallas import tpu as pltpu
from jax.sharding import PartitionSpec as P

MESH = pl.DeviceIdType.MESH
COURANT = 0.05
CENTRAL = {-3: -1, -2: 9, -1: -45, 1: 45, 2: -9, 3: 1}
DAMPING = {-3: -1, -2: 6, -1: -15, 0: 20, 1: -15, 2: 6, 3: -1}
DEN = math.exp(2.0) - 1.0
F32 = jnp.float32
BF16 = jnp.bfloat16
PARTS = 3


def stencil_matrices(cols, planes):
    tables = (CENTRAL, DAMPING, CENTRAL, DAMPING)
    rows = 128 // planes
    mx = np.zeros((6, cols, 4, 6, cols), np.float32)
    mz = np.zeros((4, 128, 128), np.float32)
    my = np.zeros((3, 4, 128, 128), np.float32)
    groups = 24 // PARTS
    mh = np.zeros((groups, cols, 2, 4, groups, 3), np.float32)
    for s, table in enumerate(tables):
        for d, coef in table.items():
            for i in range(cols):
                k = i + d
                if 0 <= k < cols:
                    for v in range(6):
                        mx[v, i, s, v, k] = coef
                elif k < 0:
                    for g in range(groups):
                        mh[g, i, 0, s, g, k + 3] = coef
                else:
                    for g in range(groups):
                        mh[g, i, 1, s, g, k - cols] = coef
            for lane in range(128):
                b, z = divmod(lane, planes)
                mz[s, b * planes + (z + d) % planes, lane] += coef
                delta, src = divmod(b + d, rows)
                my[delta + 1, s, src * planes + z, lane] += coef
    return (
        mx.reshape(6 * cols, 24 * cols),
        mz.reshape(512, 128),
        my.reshape(3, 512, 128),
        mh.reshape(groups * cols, 24 * groups),
    )


def primitives(q):
    r = 1.0 / q[0]
    u, v, w = q[1] * r, q[2] * r, q[3] * r
    p = 0.4 * (q[4] - 0.5 * (q[1] * u + q[2] * v + q[3] * w) - q[5])
    c2 = 1.4 * p * r
    return r, u, v, w, p, c2 * lax.rsqrt(c2)


def split(x):
    hi = x.astype(BF16)
    return hi, (x - hi.astype(F32)).astype(BF16)


def kernel(
    n_gx, n_gy, planes,
    q_ref, h_ref, ws_ref, sl_ref, bt_ref, mx_hbm, mz_hbm, my_hbm, mh_hbm,
    out_ref, shock_ref,
    send_lo, send_hi, recv_lo, recv_hi, hx, below, above, top,
    rx, zs, ys, keep, rh, mx, mz, my, mh, blow,
    mat_sem, s_lo, s_hi, r_lo, r_hi, hs_sem, hr_sem, ys_sem, yr_sem, ts_sem, tr_sem,
):
    cols, length = q_ref.shape[1], q_ref.shape[2]
    tiles = length // 128
    per_tile = 128 // planes
    total_rows = n_gy * (length // planes)
    dt = COURANT / total_rows
    ix, iy = lax.axis_index("gx"), lax.axis_index("gy")
    last = tiles * 128 - 128
    groups = tiles // PARTS
    has_l, has_r = ix > 0, ix < n_gx - 1
    has_b, has_a = iy > 0, iy < n_gy - 1
    is_top = iy == n_gy - 1

    mats = [
        pltpu.make_async_copy(a, b, mat_sem.at[i])
        for i, (a, b) in enumerate(((mx_hbm, mx), (mz_hbm, mz), (my_hbm, my), (mh_hbm, mh)))
    ]
    for m in mats:
        m.start()

    barrier = pltpu.get_barrier_semaphore()
    count = has_l.astype(jnp.int32) + has_r.astype(jnp.int32)

    @pl.when(has_l)
    def _():
        pl.semaphore_signal(barrier, inc=1, device_id=(ix - 1, iy), device_id_type=MESH)

    @pl.when(has_r)
    def _():
        pl.semaphore_signal(barrier, inc=1, device_id=(ix + 1, iy), device_id_type=MESH)

    for d in range(n_gy):
        near = (iy - d == 1) | (d - iy == 1) | ((iy != d) & (is_top | (d == n_gy - 1)))
        count = count + near.astype(jnp.int32)

        @pl.when(near)
        def _(d=d):
            pl.semaphore_signal(barrier, inc=1, device_id=(ix, d), device_id_type=MESH)

    for b in range(per_tile):
        hx[8 : 8 + cols, b * planes : (b + 1) * planes] = h_ref[...]

    def lanes(g, k):
        return slice((g * PARTS + k) * 128, (g * PARTS + k) * 128 + 128)

    def pack(k):
        for v in range(6):
            for g in range(groups):
                at = (v * groups + g) * 3
                send_lo[k, at : at + 3, :] = q_ref[v, 0:3, lanes(g, k)]
                send_hi[k, at : at + 3, :] = q_ref[v, cols - 3 : cols, lanes(g, k)]

    def to_left(k):
        return pltpu.make_async_remote_copy(
            send_lo.at[k], recv_hi.at[k], s_lo.at[k], r_hi.at[k],
            device_id=(ix - 1, iy), device_id_type=MESH)

    def to_right(k):
        return pltpu.make_async_remote_copy(
            send_hi.at[k], recv_lo.at[k], s_hi.at[k], r_lo.at[k],
            device_id=(ix + 1, iy), device_id_type=MESH)

    h_left = pltpu.make_async_remote_copy(
        hx.at[8:16], hx.at[8 + cols : 16 + cols], hs_sem.at[0], hr_sem.at[1],
        device_id=(ix - 1, iy), device_id_type=MESH)
    h_right = pltpu.make_async_remote_copy(
        hx.at[cols : 8 + cols], hx.at[0:8], hs_sem.at[1], hr_sem.at[0],
        device_id=(ix + 1, iy), device_id_type=MESH)
    y_down = pltpu.make_async_remote_copy(
        q_ref.at[:, :, 0:128], above, ys_sem.at[0], yr_sem.at[1],
        device_id=(ix, iy - 1), device_id_type=MESH)
    y_up = pltpu.make_async_remote_copy(
        q_ref.at[:, :, last : last + 128], below, ys_sem.at[1], yr_sem.at[0],
        device_id=(ix, iy + 1), device_id_type=MESH)

    def top_to(d):
        return pltpu.make_async_remote_copy(
            q_ref.at[:, :, last : last + 128], top, ts_sem.at[d], tr_sem,
            device_id=(ix, d), device_id_type=MESH)

    pack(0)
    pl.semaphore_wait(barrier, count)

    @pl.when(has_l)
    def _():
        h_left.start()
        to_left(0).start()

    @pl.when(has_r)
    def _():
        h_right.start()
        to_right(0).start()

    @pl.when(is_top)
    def _():
        for d in range(n_gy - 1):
            top_to(d).start()

    @pl.when(has_b)
    def _():
        y_down.start()

    @pl.when(has_a)
    def _():
        y_up.start()

    for k in range(1, PARTS):
        pack(k)

        @pl.when(has_l)
        def _(k=k):
            to_left(k).start()

        @pl.when(has_r)
        def _(k=k):
            to_right(k).start()

    @pl.when(jnp.logical_not(has_l))
    def _():
        hx[0:8, :] = jnp.broadcast_to(hx[8:9, :], (8, 128))
        for k in range(PARTS):
            for v in range(6):
                for g in range(groups):
                    at = (v * groups + g) * 3
                    recv_lo[k, at : at + 3, :] = jnp.broadcast_to(q_ref[v, 0:1, lanes(g, k)], (3, 128))

    @pl.when(jnp.logical_not(has_r))
    def _():
        hx[8 + cols : 16 + cols, :] = jnp.broadcast_to(hx[7 + cols : 8 + cols, :], (8, 128))
        for k in range(PARTS):
            for v in range(6):
                for g in range(groups):
                    at = (v * groups + g) * 3
                    recv_hi[k, at : at + 3, :] = jnp.broadcast_to(
                        q_ref[v, cols - 1 : cols, lanes(g, k)], (3, 128))

    for i in range(cols):
        row = bt_ref[pl.ds(sl_ref[ws_ref[i]], 1), :]
        for b in range(per_tile):
            blow[i : i + 1, b * planes : (b + 1) * planes] = row

    wide = 256
    halves = wide // 128
    height = hx[8 : 8 + cols, :]
    height_w = jnp.concatenate([height] * halves, axis=1)

    def phase_a(t, _):
        at = pl.ds(pl.multiple_of(t * wide, wide), wide)
        q = [q_ref[v, :, at] for v in range(6)]
        r, u, v, w, p, c = primitives(q)
        keep[0, :, at] = r
        keep[1, :, at] = p
        keep[2, :, at] = c
        rp = 1.0 / p
        inv_t = q[0] * rp
        eq = 3.0 / (jnp.exp(3.0 * inv_t) - 1.0)
        keep[3, :, at] = (q[0] * eq - q[5]) * p * (500.0 * jnp.exp(-jnp.exp(jnp.log(inv_t) * (1.0 / 3.0))))
        hc = height_w * c
        hp = height_w * p
        for axis, vel in ((0, u), (1, w)):
            hv = height_w * vel
            speed = jnp.abs(hv) + hc
            for n in range(6):
                flux = hv * q[n]
                if n == (1, 3)[axis]:
                    flux = flux + hp
                if n == 4:
                    flux = flux + hv * p
                for s, x in ((0, flux), (1, speed * q[n])):
                    for lo, y in enumerate(split(x)):
                        slab = s + 2 * lo
                        if axis == 0:
                            rx[pl.ds((slab * 6 + n) * cols, cols), at] = y
                        else:
                            for b in range(halves):
                                zs[t * halves + b, pl.ds(n * cols, cols), pl.ds(slab * 128, 128)] = (
                                    y[:, b * 128 : (b + 1) * 128])
        return 0

    lax.fori_loop(0, length // wide, phase_a, 0)

    @pl.when(has_l)
    def _():
        h_right.wait_recv()

    @pl.when(has_r)
    def _():
        h_left.wait_recv()

    @pl.when(jnp.logical_not(is_top))
    def _():
        top_to(0).wait_recv()

    @pl.when(is_top)
    def _():
        top[...] = q_ref[:, :, last : last + 128]

    slope_x = (hx[6 : 6 + cols, :] - 8.0 * hx[7 : 7 + cols, :] + 8.0 * hx[9 : 9 + cols, :]
               - hx[10 : 10 + cols, :]) / 0.6
    slope_z = (pltpu.roll(height, 2, 1) - 8.0 * pltpu.roll(height, 1, 1)
               + 8.0 * pltpu.roll(height, 127, 1) - pltpu.roll(height, 126, 1)) / 0.6
    for v in range(6):
        for b in range(per_tile - 1):
            top[v, :, b * planes : (b + 1) * planes] = top[v, :, 128 - planes : 128]
    tq = [top[v] for v in range(6)]
    r, u, v, w, p, c = primitives(tq)
    slope_sq = slope_x * slope_x + slope_z * slope_z
    g2 = 1.0 + slope_sq
    g = jnp.sqrt(g2)
    pj = 0.1 * (1.0 + 2.8 / 2.4 * (36.0 * slope_x * slope_x / g2 - 1.0))
    rate = (v - u * slope_x - w * slope_z) + g * (pj - p) * r / c
    shock_ref[...] = h_ref[...] + dt * rate[:, 0:planes]

    @pl.when(has_b)
    def _():
        y_up.wait_recv()

    @pl.when(has_a)
    def _():
        y_down.wait_recv()

    @pl.when(jnp.logical_not(has_b))
    def _():
        for v in range(6):
            for b in range(per_tile):
                below[v, :, b * planes : (b + 1) * planes] = (
                    q_ref[v, :, 128 - (b + 1) * planes : 128 - b * planes])
        old = below[2]
        blown = 2.0 * blow[...] - old
        below[2] = blown
        below[4] = below[4] + 0.5 * (blown * blown - old * old) / below[0]

    @pl.when(is_top)
    def _():
        above[...] = top[...]

    first_row = iy * (length // planes)

    def growth(tile, width):
        row = first_row + tile * per_tile + lax.broadcasted_iota(jnp.int32, (1, width), 1) // planes
        return jnp.exp(2.0 * (row.astype(F32) + 0.5) / total_rows)

    def y_flux(tile, width, q, u, v, w, p, c):
        reps = width // 128
        def rep(x):
            return x if reps == 1 else jnp.concatenate([x] * reps, axis=1)
        eta = (growth(tile, width) - 1.0) * (1.0 / DEN)
        kx, kz, kt = -eta * rep(slope_x), -eta * rep(slope_z), -eta * rep(rate)
        uc = kt + kx * u + v + kz * w
        nrm = 1.0 + eta * eta * rep(slope_sq)
        speed = jnp.abs(uc) + c * (nrm * lax.rsqrt(nrm))
        extra = {1: kx * p, 2: p, 3: kz * p, 4: p * (uc - kt)}
        for n in range(6):
            flux = q[n] * uc
            if n in extra:
                flux = flux + extra[n]
            for s, x in ((0, flux), (1, speed * q[n])):
                for lo, y in enumerate(split(x)):
                    slab = s + 2 * lo
                    for b in range(reps):
                        ys[tile + 1 + b, pl.ds(n * cols, cols), pl.ds(slab * 128, 128)] = (
                            y[:, b * 128 : (b + 1) * 128])

    for ref, tile in ((below, -1), (above, tiles)):
        gq = [ref[v] for v in range(6)]
        gr, gu, gv, gw, gp, gc = primitives(gq)
        y_flux(tile, 128, gq, gu, gv, gw, gp, gc)

    def phase_b(t, _):
        at = pl.ds(pl.multiple_of(t * wide, wide), wide)
        q = [q_ref[v, :, at] for v in range(6)]
        r, p, c = keep[0, :, at], keep[1, :, at], keep[2, :, at]
        y_flux(t * halves, wide, q, q[1] * r, q[2] * r, q[3] * r, p, c)
        return 0

    lax.fori_loop(0, length // wide, phase_b, 0)

    for m in mats:
        m.wait()

    inv_h = 1.0 / height
    scale = (-dt / 3.0) * inv_h
    decay = dt * rate * inv_h
    span = 4

    def dot(a, b):
        return jnp.dot(a, b, preferred_element_type=F32)

    def phase_c(gidx, _):
        t0 = gidx * span
        dx = dot(mx[...], rx[:, pl.ds(pl.multiple_of(t0 * 128, 128 * span), 128 * span)])
        dz = dot(zs[pl.ds(t0, span)].reshape(span * 6 * cols, 512), mz[...])
        dy = dot(ys[pl.ds(t0, span)].reshape(span * 6 * cols, 512), my[0])
        dy = dy + dot(ys[pl.ds(t0 + 1, span)].reshape(span * 6 * cols, 512), my[1])
        dy = dy + dot(ys[pl.ds(t0 + 2, span)].reshape(span * 6 * cols, 512), my[2])
        for b in range(span):
            at = pl.ds(pl.multiple_of((t0 + b) * 128, 128), 128)
            wy = (0.05 * total_rows * DEN / 2.0) / growth(t0 + b, 128)
            for v in range(6):
                lo = (b * 6 + v) * cols
                q = q_ref[v, :, at]
                d = dx[v * cols : (v + 1) * cols, b * 128 : (b + 1) * 128]
                d = d + dz[lo : lo + cols] + wy * dy[lo : lo + cols]
                new = q + scale * d - q * decay
                if v == 5:
                    new = new + dt * keep[3, :, at]
                out_ref[v, :, at] = new
        return 0

    lax.fori_loop(0, tiles // span, phase_c, 0)

    hl, hh = hx[5:8, :], hx[8 + cols : 11 + cols, :]
    heights = [jnp.concatenate([x] * groups, axis=0) for x in (hl, hh)]
    size = groups * 3
    for k in range(PARTS):
        @pl.when(has_l)
        def _(k=k):
            to_right(k).wait_recv()

        @pl.when(has_r)
        def _(k=k):
            to_left(k).wait_recv()

        for side, ref in enumerate((recv_lo, recv_hi)):
            q = [ref[k, v * size : (v + 1) * size, :] for v in range(6)]
            r, u, v, w, p, c = primitives(q)
            hv = heights[side] * u
            speed = jnp.abs(hv) + heights[side] * c
            for n in range(6):
                flux = hv * q[n]
                if n == 1:
                    flux = flux + heights[side] * p
                if n == 4:
                    flux = flux + hv * p
                fs, as_ = split(flux), split(speed * q[n])
                block = jnp.concatenate([fs[0].astype(F32), as_[0].astype(F32), fs[1].astype(F32), as_[1].astype(F32)], axis=0).astype(BF16)
                rh[side * 4 * size : (side + 1) * 4 * size, n * 128 : (n + 1) * 128] = block
        d = dot(mh[...], rh[...])
        for g in range(groups):
            for v in range(6):
                out_ref[v, :, lanes(g, k)] += scale * d[g * cols : (g + 1) * cols, v * 128 : (v + 1) * 128]

    @pl.when(has_l)
    def _():
        h_left.wait_send()
        for k in range(PARTS):
            to_left(k).wait_send()

    @pl.when(has_r)
    def _():
        h_right.wait_send()
        for k in range(PARTS):
            to_right(k).wait_send()

    @pl.when(is_top)
    def _():
        for d in range(n_gy - 1):
            top_to(d).wait_send()

    @pl.when(has_b)
    def _():
        y_down.wait_send()

    @pl.when(has_a)
    def _():
        y_up.wait_send()


def solution(mesh):
    n_gx, n_gy = mesh.shape["gx"], mesh.shape["gy"]

    def shards(state, shock_height, wall_segment, segment_level, blow_table):
        planes = blow_table.shape[1]
        cols, length = state.shape[1], state.shape[2]
        tiles = length // 128
        groups = tiles // PARTS
        mats = [jnp.asarray(m, BF16) for m in stencil_matrices(cols, planes)]
        vmem = pl.BlockSpec(memory_space=pltpu.VMEM)
        smem = pl.BlockSpec(memory_space=pltpu.SMEM)
        hbm = pl.BlockSpec(memory_space=pl.ANY)
        packed = pltpu.VMEM((PARTS, 18 * groups, 128), F32)
        tile6 = pltpu.VMEM((6, cols, 128), F32)
        sem = pltpu.SemaphoreType.DMA
        return pl.pallas_call(
            functools.partial(kernel, n_gx, n_gy, planes),
            out_shape=(
                jax.ShapeDtypeStruct(state.shape, F32),
                jax.ShapeDtypeStruct(shock_height.shape, F32),
            ),
            in_specs=[vmem, vmem, smem, smem, vmem, hbm, hbm, hbm, hbm],
            out_specs=(vmem, vmem),
            scratch_shapes=[
                packed, packed, packed, packed,
                pltpu.VMEM((16 + cols, 128), F32),
                tile6, tile6, tile6,
                pltpu.VMEM((24 * cols, length), BF16),
                pltpu.VMEM((tiles, 6 * cols, 512), BF16),
                pltpu.VMEM((tiles + 2, 6 * cols, 512), BF16),
                pltpu.VMEM((4, cols, length), F32),
                pltpu.VMEM((24 * groups, 768), BF16),
                *[pltpu.VMEM(m.shape, BF16) for m in mats],
                pltpu.VMEM((cols, 128), F32),
                sem((4,)), sem((PARTS,)), sem((PARTS,)), sem((PARTS,)), sem((PARTS,)),
                sem((2,)), sem((2,)), sem((2,)), sem((2,)), sem((n_gy,)), sem,
            ],
            compiler_params=pltpu.CompilerParams(
                collective_id=0, has_side_effects=True, vmem_limit_bytes=40 * 1024 * 1024),
        )(state, shock_height, wall_segment, segment_level, blow_table, *mats)

    in_specs = (P(None, "gx", "gy"), P("gx", None), P("gx"), P(), P())
    out_specs = (P(None, "gx", "gy"), P("gx", None))
    return jax.shard_map(shards, mesh=mesh, in_specs=in_specs, out_specs=out_specs, check_vma=False)
```

```python
import functools
import math

import jax
import jax.numpy as jnp
import numpy as np
from jax import lax
from jax.experimental import pallas as pl
from jax.experimental.pallas import tpu as pltpu
from jax.sharding import PartitionSpec as P

MESH = pl.DeviceIdType.MESH
COURANT = 0.05
CENTRAL = {-3: -1, -2: 9, -1: -45, 1: 45, 2: -9, 3: 1}
DAMPING = {-3: -1, -2: 6, -1: -15, 0: 20, 1: -15, 2: 6, 3: -1}
DEN = math.exp(2.0) - 1.0
F32 = jnp.float32
BF16 = jnp.bfloat16
PARTS = 3


def stencil_matrices(cols, planes):
    tables = (CENTRAL, DAMPING, CENTRAL, DAMPING)
    rows = 128 // planes
    mx = np.zeros((6, cols, 4, 6, cols), np.float32)
    mz = np.zeros((4, 128, 128), np.float32)
    my = np.zeros((3, 4, 128, 128), np.float32)
    groups = 24 // PARTS
    mh = np.zeros((groups, cols, 2, 4, groups, 3), np.float32)
    for s, table in enumerate(tables):
        for d, coef in table.items():
            for i in range(cols):
                k = i + d
                if 0 <= k < cols:
                    for v in range(6):
                        mx[v, i, s, v, k] = coef
                elif k < 0:
                    for g in range(groups):
                        mh[g, i, 0, s, g, k + 3] = coef
                else:
                    for g in range(groups):
                        mh[g, i, 1, s, g, k - cols] = coef
            for lane in range(128):
                b, z = divmod(lane, planes)
                mz[s, b * planes + (z + d) % planes, lane] += coef
                delta, src = divmod(b + d, rows)
                my[delta + 1, s, src * planes + z, lane] += coef
    return (
        mx.reshape(6 * cols, 24 * cols),
        mz.reshape(512, 128),
        my.reshape(3, 512, 128),
        mh.reshape(groups * cols, 24 * groups),
    )


def primitives(q):
    r = 1.0 / q[0]
    u, v, w = q[1] * r, q[2] * r, q[3] * r
    p = 0.4 * (q[4] - 0.5 * (q[1] * u + q[2] * v + q[3] * w) - q[5])
    c2 = 1.4 * p * r
    return r, u, v, w, p, c2 * lax.rsqrt(c2)


def split(x):
    hi = x.astype(BF16)
    return hi, (x - hi.astype(F32)).astype(BF16)


def kernel(
    n_gx, n_gy, planes,
    q_hbm, h_hbm, ws_hbm, sl_hbm, bt_hbm, mx_hbm, mz_hbm, my_hbm, mh_hbm,
    out_ref, shock_ref,
    q_ref, h_ref, ws_ref, sl_ref, bt_ref,
    send_lo, send_hi, recv_lo, recv_hi, hx, below, above, top,
    rx, zs, ys, keep, rh, mx, mz, my, mh, blow,
    mat_sem, s_lo, s_hi, r_lo, r_hi, hs_sem, hr_sem, ys_sem, yr_sem, ts_sem, tr_sem,
):
    cols, length = q_hbm.shape[1], q_hbm.shape[2]
    tiles = length // 128
    per_tile = 128 // planes
    total_rows = n_gy * (length // planes)
    dt = COURANT / total_rows
    ix, iy = lax.axis_index("gx"), lax.axis_index("gy")
    last = tiles * 128 - 128
    groups = tiles // PARTS
    has_l, has_r = ix > 0, ix < n_gx - 1
    has_b, has_a = iy > 0, iy < n_gy - 1
    is_top = iy == n_gy - 1

    mats = [
        pltpu.make_async_copy(a, b, mat_sem.at[i])
        for i, (a, b) in enumerate((
            (q_hbm, q_ref), (h_hbm, h_ref), (ws_hbm, ws_ref), (sl_hbm, sl_ref), (bt_hbm, bt_ref),
            (mx_hbm, mx), (mz_hbm, mz), (my_hbm, my), (mh_hbm, mh)))
    ]
    for m in mats[:2]:
        m.start()

    barrier = pltpu.get_barrier_semaphore()
    count = has_l.astype(jnp.int32) + has_r.astype(jnp.int32)

    @pl.when(has_l)
    def _():
        pl.semaphore_signal(barrier, inc=1, device_id=(ix - 1, iy), device_id_type=MESH)

    @pl.when(has_r)
    def _():
        pl.semaphore_signal(barrier, inc=1, device_id=(ix + 1, iy), device_id_type=MESH)

    for d in range(n_gy):
        near = (iy - d == 1) | (d - iy == 1) | ((iy != d) & (is_top | (d == n_gy - 1)))
        count = count + near.astype(jnp.int32)

        @pl.when(near)
        def _(d=d):
            pl.semaphore_signal(barrier, inc=1, device_id=(ix, d), device_id_type=MESH)

    for m in mats[2:]:
        m.start()
    for m in mats[:2]:
        m.wait()

    for b in range(per_tile):
        hx[8 : 8 + cols, b * planes : (b + 1) * planes] = h_ref[...]

    def lanes(g, k):
        return slice((g * PARTS + k) * 128, (g * PARTS + k) * 128 + 128)

    def pack(k):
        for v in range(6):
            for g in range(groups):
                at = (v * groups + g) * 3
                send_lo[k, at : at + 3, :] = q_ref[v, 0:3, lanes(g, k)]
                send_hi[k, at : at + 3, :] = q_ref[v, cols - 3 : cols, lanes(g, k)]

    def to_left(k):
        return pltpu.make_async_remote_copy(
            send_lo.at[k], recv_hi.at[k], s_lo.at[k], r_hi.at[k],
            device_id=(ix - 1, iy), device_id_type=MESH)

    def to_right(k):
        return pltpu.make_async_remote_copy(
            send_hi.at[k], recv_lo.at[k], s_hi.at[k], r_lo.at[k],
            device_id=(ix + 1, iy), device_id_type=MESH)

    h_left = pltpu.make_async_remote_copy(
        hx.at[8:16], hx.at[8 + cols : 16 + cols], hs_sem.at[0], hr_sem.at[1],
        device_id=(ix - 1, iy), device_id_type=MESH)
    h_right = pltpu.make_async_remote_copy(
        hx.at[cols : 8 + cols], hx.at[0:8], hs_sem.at[1], hr_sem.at[0],
        device_id=(ix + 1, iy), device_id_type=MESH)
    y_down = pltpu.make_async_remote_copy(
        q_ref.at[:, :, 0:128], above, ys_sem.at[0], yr_sem.at[1],
        device_id=(ix, iy - 1), device_id_type=MESH)
    y_up = pltpu.make_async_remote_copy(
        q_ref.at[:, :, last : last + 128], below, ys_sem.at[1], yr_sem.at[0],
        device_id=(ix, iy + 1), device_id_type=MESH)

    def top_to(d):
        return pltpu.make_async_remote_copy(
            q_ref.at[:, :, last : last + 128], top, ts_sem.at[d], tr_sem,
            device_id=(ix, d), device_id_type=MESH)

    pack(0)
    pl.semaphore_wait(barrier, count)

    @pl.when(has_l)
    def _():
        h_left.start()
        to_left(0).start()

    @pl.when(has_r)
    def _():
        h_right.start()
        to_right(0).start()

    @pl.when(is_top)
    def _():
        for d in range(n_gy - 1):
            top_to(d).start()

    @pl.when(has_b)
    def _():
        y_down.start()

    @pl.when(has_a)
    def _():
        y_up.start()

    for k in range(1, PARTS):
        pack(k)

        @pl.when(has_l)
        def _(k=k):
            to_left(k).start()

        @pl.when(has_r)
        def _(k=k):
            to_right(k).start()

    @pl.when(jnp.logical_not(has_l))
    def _():
        hx[0:8, :] = jnp.broadcast_to(hx[8:9, :], (8, 128))
        for k in range(PARTS):
            for v in range(6):
                for g in range(groups):
                    at = (v * groups + g) * 3
                    recv_lo[k, at : at + 3, :] = jnp.broadcast_to(q_ref[v, 0:1, lanes(g, k)], (3, 128))

    @pl.when(jnp.logical_not(has_r))
    def _():
        hx[8 + cols : 16 + cols, :] = jnp.broadcast_to(hx[7 + cols : 8 + cols, :], (8, 128))
        for k in range(PARTS):
            for v in range(6):
                for g in range(groups):
                    at = (v * groups + g) * 3
                    recv_hi[k, at : at + 3, :] = jnp.broadcast_to(
                        q_ref[v, cols - 1 : cols, lanes(g, k)], (3, 128))

    for m in mats[2:5]:
        m.wait()

    for i in range(cols):
        row = bt_ref[pl.ds(sl_ref[ws_ref[i]], 1), :]
        for b in range(per_tile):
            blow[i : i + 1, b * planes : (b + 1) * planes] = row

    wide = 256
    halves = wide // 128
    height = hx[8 : 8 + cols, :]
    height_w = jnp.concatenate([height] * halves, axis=1)

    def phase_a(t, _):
        at = pl.ds(pl.multiple_of(t * wide, wide), wide)
        q = [q_ref[v, :, at] for v in range(6)]
        r, u, v, w, p, c = primitives(q)
        keep[0, :, at] = r
        keep[1, :, at] = p
        keep[2, :, at] = c
        rp = 1.0 / p
        inv_t = q[0] * rp
        eq = 3.0 / (jnp.exp(3.0 * inv_t) - 1.0)
        keep[3, :, at] = (q[0] * eq - q[5]) * p * (500.0 * jnp.exp(-jnp.exp(jnp.log(inv_t) * (1.0 / 3.0))))
        hc = height_w * c
        hp = height_w * p
        for axis, vel in ((0, u), (1, w)):
            hv = height_w * vel
            speed = jnp.abs(hv) + hc
            for n in range(6):
                flux = hv * q[n]
                if n == (1, 3)[axis]:
                    flux = flux + hp
                if n == 4:
                    flux = flux + hv * p
                for s, x in ((0, flux), (1, speed * q[n])):
                    for lo, y in enumerate(split(x)):
                        slab = s + 2 * lo
                        if axis == 0:
                            rx[pl.ds((slab * 6 + n) * cols, cols), at] = y
                        else:
                            for b in range(halves):
                                zs[t * halves + b, pl.ds(n * cols, cols), pl.ds(slab * 128, 128)] = (
                                    y[:, b * 128 : (b + 1) * 128])
        return 0

    lax.fori_loop(0, length // wide, phase_a, 0)

    @pl.when(has_l)
    def _():
        h_right.wait_recv()

    @pl.when(has_r)
    def _():
        h_left.wait_recv()

    @pl.when(jnp.logical_not(is_top))
    def _():
        top_to(0).wait_recv()

    @pl.when(is_top)
    def _():
        top[...] = q_ref[:, :, last : last + 128]

    slope_x = (hx[6 : 6 + cols, :] - 8.0 * hx[7 : 7 + cols, :] + 8.0 * hx[9 : 9 + cols, :]
               - hx[10 : 10 + cols, :]) / 0.6
    slope_z = (pltpu.roll(height, 2, 1) - 8.0 * pltpu.roll(height, 1, 1)
               + 8.0 * pltpu.roll(height, 127, 1) - pltpu.roll(height, 126, 1)) / 0.6
    for v in range(6):
        for b in range(per_tile - 1):
            top[v, :, b * planes : (b + 1) * planes] = top[v, :, 128 - planes : 128]
    tq = [top[v] for v in range(6)]
    r, u, v, w, p, c = primitives(tq)
    slope_sq = slope_x * slope_x + slope_z * slope_z
    g2 = 1.0 + slope_sq
    g = jnp.sqrt(g2)
    pj = 0.1 * (1.0 + 2.8 / 2.4 * (36.0 * slope_x * slope_x / g2 - 1.0))
    rate = (v - u * slope_x - w * slope_z) + g * (pj - p) * r / c
    shock_ref[...] = h_ref[...] + dt * rate[:, 0:planes]

    @pl.when(has_b)
    def _():
        y_up.wait_recv()

    @pl.when(has_a)
    def _():
        y_down.wait_recv()

    @pl.when(jnp.logical_not(has_b))
    def _():
        for v in range(6):
            for b in range(per_tile):
                below[v, :, b * planes : (b + 1) * planes] = (
                    q_ref[v, :, 128 - (b + 1) * planes : 128 - b * planes])
        old = below[2]
        blown = 2.0 * blow[...] - old
        below[2] = blown
        below[4] = below[4] + 0.5 * (blown * blown - old * old) / below[0]

    @pl.when(is_top)
    def _():
        above[...] = top[...]

    first_row = iy * (length // planes)

    def growth(tile, width):
        row = first_row + tile * per_tile + lax.broadcasted_iota(jnp.int32, (1, width), 1) // planes
        return jnp.exp(2.0 * (row.astype(F32) + 0.5) / total_rows)

    def y_flux(tile, width, q, u, v, w, p, c):
        reps = width // 128
        def rep(x):
            return x if reps == 1 else jnp.concatenate([x] * reps, axis=1)
        eta = (growth(tile, width) - 1.0) * (1.0 / DEN)
        kx, kz, kt = -eta * rep(slope_x), -eta * rep(slope_z), -eta * rep(rate)
        uc = kt + kx * u + v + kz * w
        nrm = 1.0 + eta * eta * rep(slope_sq)
        speed = jnp.abs(uc) + c * (nrm * lax.rsqrt(nrm))
        extra = {1: kx * p, 2: p, 3: kz * p, 4: p * (uc - kt)}
        for n in range(6):
            flux = q[n] * uc
            if n in extra:
                flux = flux + extra[n]
            for s, x in ((0, flux), (1, speed * q[n])):
                for lo, y in enumerate(split(x)):
                    slab = s + 2 * lo
                    for b in range(reps):
                        ys[tile + 1 + b, pl.ds(n * cols, cols), pl.ds(slab * 128, 128)] = (
                            y[:, b * 128 : (b + 1) * 128])

    for ref, tile in ((below, -1), (above, tiles)):
        gq = [ref[v] for v in range(6)]
        gr, gu, gv, gw, gp, gc = primitives(gq)
        y_flux(tile, 128, gq, gu, gv, gw, gp, gc)

    def phase_b(t, _):
        at = pl.ds(pl.multiple_of(t * wide, wide), wide)
        q = [q_ref[v, :, at] for v in range(6)]
        r, p, c = keep[0, :, at], keep[1, :, at], keep[2, :, at]
        y_flux(t * halves, wide, q, q[1] * r, q[2] * r, q[3] * r, p, c)
        return 0

    lax.fori_loop(0, length // wide, phase_b, 0)

    for m in mats[5:]:
        m.wait()

    inv_h = 1.0 / height
    scale = (-dt / 3.0) * inv_h
    decay = dt * rate * inv_h
    span = 4

    def dot(a, b):
        return jnp.dot(a, b, preferred_element_type=F32)

    def phase_c(gidx, _):
        t0 = gidx * span
        dx = dot(mx[...], rx[:, pl.ds(pl.multiple_of(t0 * 128, 128 * span), 128 * span)])
        dz = dot(zs[pl.ds(t0, span)].reshape(span * 6 * cols, 512), mz[...])
        dy = dot(ys[pl.ds(t0, span)].reshape(span * 6 * cols, 512), my[0])
        dy = dy + dot(ys[pl.ds(t0 + 1, span)].reshape(span * 6 * cols, 512), my[1])
        dy = dy + dot(ys[pl.ds(t0 + 2, span)].reshape(span * 6 * cols, 512), my[2])
        for b in range(span):
            at = pl.ds(pl.multiple_of((t0 + b) * 128, 128), 128)
            wy = (0.05 * total_rows * DEN / 2.0) / growth(t0 + b, 128)
            for v in range(6):
                lo = (b * 6 + v) * cols
                q = q_ref[v, :, at]
                d = dx[v * cols : (v + 1) * cols, b * 128 : (b + 1) * 128]
                d = d + dz[lo : lo + cols] + wy * dy[lo : lo + cols]
                new = q + scale * d - q * decay
                if v == 5:
                    new = new + dt * keep[3, :, at]
                out_ref[v, :, at] = new
        return 0

    lax.fori_loop(0, tiles // span, phase_c, 0)

    hl, hh = hx[5:8, :], hx[8 + cols : 11 + cols, :]
    heights = [jnp.concatenate([x] * groups, axis=0) for x in (hl, hh)]
    size = groups * 3
    for k in range(PARTS):
        @pl.when(has_l)
        def _(k=k):
            to_right(k).wait_recv()

        @pl.when(has_r)
        def _(k=k):
            to_left(k).wait_recv()

        for side, ref in enumerate((recv_lo, recv_hi)):
            q = [ref[k, v * size : (v + 1) * size, :] for v in range(6)]
            r, u, v, w, p, c = primitives(q)
            hv = heights[side] * u
            speed = jnp.abs(hv) + heights[side] * c
            for n in range(6):
                flux = hv * q[n]
                if n == 1:
                    flux = flux + heights[side] * p
                if n == 4:
                    flux = flux + hv * p
                fs, as_ = split(flux), split(speed * q[n])
                block = jnp.concatenate([fs[0].astype(F32), as_[0].astype(F32), fs[1].astype(F32), as_[1].astype(F32)], axis=0).astype(BF16)
                rh[side * 4 * size : (side + 1) * 4 * size, n * 128 : (n + 1) * 128] = block
        d = dot(mh[...], rh[...])
        for g in range(groups):
            for v in range(6):
                out_ref[v, :, lanes(g, k)] += scale * d[g * cols : (g + 1) * cols, v * 128 : (v + 1) * 128]

    @pl.when(has_l)
    def _():
        h_left.wait_send()
        for k in range(PARTS):
            to_left(k).wait_send()

    @pl.when(has_r)
    def _():
        h_right.wait_send()
        for k in range(PARTS):
            to_right(k).wait_send()

    @pl.when(is_top)
    def _():
        for d in range(n_gy - 1):
            top_to(d).wait_send()

    @pl.when(has_b)
    def _():
        y_down.wait_send()

    @pl.when(has_a)
    def _():
        y_up.wait_send()


def solution(mesh):
    n_gx, n_gy = mesh.shape["gx"], mesh.shape["gy"]

    def shards(state, shock_height, wall_segment, segment_level, blow_table):
        planes = blow_table.shape[1]
        cols, length = state.shape[1], state.shape[2]
        tiles = length // 128
        groups = tiles // PARTS
        mats = [jnp.asarray(m, BF16) for m in stencil_matrices(cols, planes)]
        vmem = pl.BlockSpec(memory_space=pltpu.VMEM)
        hbm = pl.BlockSpec(memory_space=pltpu.HBM)
        packed = pltpu.VMEM((PARTS, 18 * groups, 128), F32)
        tile6 = pltpu.VMEM((6, cols, 128), F32)
        sem = pltpu.SemaphoreType.DMA
        return pl.pallas_call(
            functools.partial(kernel, n_gx, n_gy, planes),
            out_shape=(
                jax.ShapeDtypeStruct(state.shape, F32),
                jax.ShapeDtypeStruct(shock_height.shape, F32),
            ),
            in_specs=[hbm] * 9,
            out_specs=(vmem, vmem),
            scratch_shapes=[
                pltpu.VMEM(state.shape, F32),
                pltpu.VMEM(shock_height.shape, F32),
                pltpu.SMEM(wall_segment.shape, jnp.int32),
                pltpu.SMEM(segment_level.shape, jnp.int32),
                pltpu.VMEM(blow_table.shape, F32),
                packed, packed, packed, packed,
                pltpu.VMEM((16 + cols, 128), F32),
                tile6, tile6, tile6,
                pltpu.VMEM((24 * cols, length), BF16),
                pltpu.VMEM((tiles, 6 * cols, 512), BF16),
                pltpu.VMEM((tiles + 2, 6 * cols, 512), BF16),
                pltpu.VMEM((4, cols, length), F32),
                pltpu.VMEM((24 * groups, 768), BF16),
                *[pltpu.VMEM(m.shape, BF16) for m in mats],
                pltpu.VMEM((cols, 128), F32),
                sem((9,)), sem((PARTS,)), sem((PARTS,)), sem((PARTS,)), sem((PARTS,)),
                sem((2,)), sem((2,)), sem((2,)), sem((2,)), sem((n_gy,)), sem,
            ],
            compiler_params=pltpu.CompilerParams(
                collective_id=0, has_side_effects=True, vmem_limit_bytes=62 * 1024 * 1024),
        )(state, shock_height, wall_segment, segment_level, blow_table, *mats)

    in_specs = (P(None, "gx", "gy"), P("gx", None), P("gx"), P(), P())
    out_specs = (P(None, "gx", "gy"), P("gx", None))
    return jax.shard_map(shards, mesh=mesh, in_specs=in_specs, out_specs=out_specs, check_vma=False)
```

```python
import functools
import math

import jax
import jax.numpy as jnp
import numpy as np
from jax import lax
from jax.experimental import pallas as pl
from jax.experimental.pallas import tpu as pltpu
from jax.sharding import PartitionSpec as P

MESH = pl.DeviceIdType.MESH
COURANT = 0.05
CENTRAL = {-3: -1, -2: 9, -1: -45, 1: 45, 2: -9, 3: 1}
DAMPING = {-3: -1, -2: 6, -1: -15, 0: 20, 1: -15, 2: 6, 3: -1}
DEN = math.exp(2.0) - 1.0
F32 = jnp.float32
BF16 = jnp.bfloat16
PARTS = 3


def stencil_matrices(cols, planes):
    tables = (CENTRAL, DAMPING, CENTRAL, DAMPING)
    rows = 128 // planes
    mx = np.zeros((6, cols, 4, 6, cols), np.float32)
    mz = np.zeros((4, 128, 128), np.float32)
    my = np.zeros((3, 4, 128, 128), np.float32)
    groups = 24 // PARTS
    mh = np.zeros((groups, cols, 2, 4, groups, 3), np.float32)
    for s, table in enumerate(tables):
        for d, coef in table.items():
            for i in range(cols):
                k = i + d
                if 0 <= k < cols:
                    for v in range(6):
                        mx[v, i, s, v, k] = coef
                elif k < 0:
                    for g in range(groups):
                        mh[g, i, 0, s, g, k + 3] = coef
                else:
                    for g in range(groups):
                        mh[g, i, 1, s, g, k - cols] = coef
            for lane in range(128):
                b, z = divmod(lane, planes)
                mz[s, b * planes + (z + d) % planes, lane] += coef
                delta, src = divmod(b + d, rows)
                my[delta + 1, s, src * planes + z, lane] += coef
    return (
        mx.reshape(6 * cols, 24 * cols),
        mz.reshape(512, 128),
        my.reshape(3, 512, 128),
        mh.reshape(groups * cols, 24 * groups),
    )


def primitives(q):
    r = 1.0 / q[0]
    u, v, w = q[1] * r, q[2] * r, q[3] * r
    p = 0.4 * (q[4] - 0.5 * (q[1] * u + q[2] * v + q[3] * w) - q[5])
    c2 = 1.4 * p * r
    return r, u, v, w, p, c2 * lax.rsqrt(c2)


def split(x):
    hi = x.astype(BF16)
    return hi, (x - hi.astype(F32)).astype(BF16)


def kernel(
    n_gx, n_gy, planes,
    q_hbm, h_hbm, ws_hbm, sl_hbm, bt_hbm, mx_hbm, mz_hbm, my_hbm, mh_hbm,
    out_hbm, shock_ref,
    out_ref, q_ref, h_ref, ws_ref, sl_ref, bt_ref,
    send_lo, send_hi, recv_lo, recv_hi, hx, below, above, top,
    rx, zs, ys, keep, rh, mx, mz, my, mh, blow,
    mat_sem, out_sem, s_lo, s_hi, r_lo, r_hi, hs_sem, hr_sem, ys_sem, yr_sem, ts_sem, tr_sem,
):
    cols, length = q_hbm.shape[1], q_hbm.shape[2]
    tiles = length // 128
    per_tile = 128 // planes
    total_rows = n_gy * (length // planes)
    dt = COURANT / total_rows
    ix, iy = lax.axis_index("gx"), lax.axis_index("gy")
    last = tiles * 128 - 128
    groups = tiles // PARTS
    has_l, has_r = ix > 0, ix < n_gx - 1
    has_b, has_a = iy > 0, iy < n_gy - 1
    is_top = iy == n_gy - 1

    mats = [
        pltpu.make_async_copy(a, b, mat_sem.at[i])
        for i, (a, b) in enumerate((
            (q_hbm, q_ref), (h_hbm, h_ref), (ws_hbm, ws_ref), (sl_hbm, sl_ref), (bt_hbm, bt_ref),
            (mx_hbm, mx), (mz_hbm, mz), (my_hbm, my), (mh_hbm, mh)))
    ]
    for m in mats[:2]:
        m.start()

    barrier = pltpu.get_barrier_semaphore()
    count = has_l.astype(jnp.int32) + has_r.astype(jnp.int32)

    @pl.when(has_l)
    def _():
        pl.semaphore_signal(barrier, inc=1, device_id=(ix - 1, iy), device_id_type=MESH)

    @pl.when(has_r)
    def _():
        pl.semaphore_signal(barrier, inc=1, device_id=(ix + 1, iy), device_id_type=MESH)

    for d in range(n_gy):
        near = (iy - d == 1) | (d - iy == 1) | ((iy != d) & (is_top | (d == n_gy - 1)))
        count = count + near.astype(jnp.int32)

        @pl.when(near)
        def _(d=d):
            pl.semaphore_signal(barrier, inc=1, device_id=(ix, d), device_id_type=MESH)

    for m in mats[2:]:
        m.start()
    for m in mats[:2]:
        m.wait()

    for b in range(per_tile):
        hx[8 : 8 + cols, b * planes : (b + 1) * planes] = h_ref[...]

    def lanes(g, k):
        return slice((g * PARTS + k) * 128, (g * PARTS + k) * 128 + 128)

    def pack(k):
        for v in range(6):
            for g in range(groups):
                at = (v * groups + g) * 3
                send_lo[k, at : at + 3, :] = q_ref[v, 0:3, lanes(g, k)]
                send_hi[k, at : at + 3, :] = q_ref[v, cols - 3 : cols, lanes(g, k)]

    def to_left(k):
        return pltpu.make_async_remote_copy(
            send_lo.at[k], recv_hi.at[k], s_lo.at[k], r_hi.at[k],
            device_id=(ix - 1, iy), device_id_type=MESH)

    def to_right(k):
        return pltpu.make_async_remote_copy(
            send_hi.at[k], recv_lo.at[k], s_hi.at[k], r_lo.at[k],
            device_id=(ix + 1, iy), device_id_type=MESH)

    h_left = pltpu.make_async_remote_copy(
        hx.at[8:16], hx.at[8 + cols : 16 + cols], hs_sem.at[0], hr_sem.at[1],
        device_id=(ix - 1, iy), device_id_type=MESH)
    h_right = pltpu.make_async_remote_copy(
        hx.at[cols : 8 + cols], hx.at[0:8], hs_sem.at[1], hr_sem.at[0],
        device_id=(ix + 1, iy), device_id_type=MESH)
    y_down = pltpu.make_async_remote_copy(
        q_ref.at[:, :, 0:128], above, ys_sem.at[0], yr_sem.at[1],
        device_id=(ix, iy - 1), device_id_type=MESH)
    y_up = pltpu.make_async_remote_copy(
        q_ref.at[:, :, last : last + 128], below, ys_sem.at[1], yr_sem.at[0],
        device_id=(ix, iy + 1), device_id_type=MESH)

    def top_to(d):
        return pltpu.make_async_remote_copy(
            q_ref.at[:, :, last : last + 128], top, ts_sem.at[d], tr_sem,
            device_id=(ix, d), device_id_type=MESH)

    pack(0)
    pl.semaphore_wait(barrier, count)

    @pl.when(has_l)
    def _():
        h_left.start()
        to_left(0).start()

    @pl.when(has_r)
    def _():
        h_right.start()
        to_right(0).start()

    @pl.when(is_top)
    def _():
        for d in range(n_gy - 1):
            top_to(d).start()

    @pl.when(has_b)
    def _():
        y_down.start()

    @pl.when(has_a)
    def _():
        y_up.start()

    for k in range(1, PARTS):
        pack(k)

        @pl.when(has_l)
        def _(k=k):
            to_left(k).start()

        @pl.when(has_r)
        def _(k=k):
            to_right(k).start()

    @pl.when(jnp.logical_not(has_l))
    def _():
        hx[0:8, :] = jnp.broadcast_to(hx[8:9, :], (8, 128))
        for k in range(PARTS):
            for v in range(6):
                for g in range(groups):
                    at = (v * groups + g) * 3
                    recv_lo[k, at : at + 3, :] = jnp.broadcast_to(q_ref[v, 0:1, lanes(g, k)], (3, 128))

    @pl.when(jnp.logical_not(has_r))
    def _():
        hx[8 + cols : 16 + cols, :] = jnp.broadcast_to(hx[7 + cols : 8 + cols, :], (8, 128))
        for k in range(PARTS):
            for v in range(6):
                for g in range(groups):
                    at = (v * groups + g) * 3
                    recv_hi[k, at : at + 3, :] = jnp.broadcast_to(
                        q_ref[v, cols - 1 : cols, lanes(g, k)], (3, 128))

    for m in mats[2:5]:
        m.wait()

    for i in range(cols):
        row = bt_ref[pl.ds(sl_ref[ws_ref[i]], 1), :]
        for b in range(per_tile):
            blow[i : i + 1, b * planes : (b + 1) * planes] = row

    wide = 256
    halves = wide // 128
    height = hx[8 : 8 + cols, :]
    height_w = jnp.concatenate([height] * halves, axis=1)

    def phase_a(t, _):
        at = pl.ds(pl.multiple_of(t * wide, wide), wide)
        q = [q_ref[v, :, at] for v in range(6)]
        r, u, v, w, p, c = primitives(q)
        keep[0, :, at] = r
        keep[1, :, at] = p
        keep[2, :, at] = c
        rp = 1.0 / p
        inv_t = q[0] * rp
        eq = 3.0 / (jnp.exp(3.0 * inv_t) - 1.0)
        keep[3, :, at] = (q[0] * eq - q[5]) * p * (500.0 * jnp.exp(-jnp.exp(jnp.log(inv_t) * (1.0 / 3.0))))
        hc = height_w * c
        hp = height_w * p
        for axis, vel in ((0, u), (1, w)):
            hv = height_w * vel
            speed = jnp.abs(hv) + hc
            for n in range(6):
                flux = hv * q[n]
                if n == (1, 3)[axis]:
                    flux = flux + hp
                if n == 4:
                    flux = flux + hv * p
                for s, x in ((0, flux), (1, speed * q[n])):
                    for lo, y in enumerate(split(x)):
                        slab = s + 2 * lo
                        if axis == 0:
                            rx[pl.ds((slab * 6 + n) * cols, cols), at] = y
                        else:
                            for b in range(halves):
                                zs[t * halves + b, pl.ds(n * cols, cols), pl.ds(slab * 128, 128)] = (
                                    y[:, b * 128 : (b + 1) * 128])
        return 0

    lax.fori_loop(0, length // wide, phase_a, 0)

    @pl.when(has_l)
    def _():
        h_right.wait_recv()

    @pl.when(has_r)
    def _():
        h_left.wait_recv()

    @pl.when(jnp.logical_not(is_top))
    def _():
        top_to(0).wait_recv()

    @pl.when(is_top)
    def _():
        top[...] = q_ref[:, :, last : last + 128]

    slope_x = (hx[6 : 6 + cols, :] - 8.0 * hx[7 : 7 + cols, :] + 8.0 * hx[9 : 9 + cols, :]
               - hx[10 : 10 + cols, :]) / 0.6
    slope_z = (pltpu.roll(height, 2, 1) - 8.0 * pltpu.roll(height, 1, 1)
               + 8.0 * pltpu.roll(height, 127, 1) - pltpu.roll(height, 126, 1)) / 0.6
    for v in range(6):
        for b in range(per_tile - 1):
            top[v, :, b * planes : (b + 1) * planes] = top[v, :, 128 - planes : 128]
    tq = [top[v] for v in range(6)]
    r, u, v, w, p, c = primitives(tq)
    slope_sq = slope_x * slope_x + slope_z * slope_z
    g2 = 1.0 + slope_sq
    g = jnp.sqrt(g2)
    pj = 0.1 * (1.0 + 2.8 / 2.4 * (36.0 * slope_x * slope_x / g2 - 1.0))
    rate = (v - u * slope_x - w * slope_z) + g * (pj - p) * r / c
    shock_ref[...] = h_ref[...] + dt * rate[:, 0:planes]

    @pl.when(has_b)
    def _():
        y_up.wait_recv()

    @pl.when(has_a)
    def _():
        y_down.wait_recv()

    @pl.when(jnp.logical_not(has_b))
    def _():
        for v in range(6):
            for b in range(per_tile):
                below[v, :, b * planes : (b + 1) * planes] = (
                    q_ref[v, :, 128 - (b + 1) * planes : 128 - b * planes])
        old = below[2]
        blown = 2.0 * blow[...] - old
        below[2] = blown
        below[4] = below[4] + 0.5 * (blown * blown - old * old) / below[0]

    @pl.when(is_top)
    def _():
        above[...] = top[...]

    first_row = iy * (length // planes)

    def growth(tile, width):
        row = first_row + tile * per_tile + lax.broadcasted_iota(jnp.int32, (1, width), 1) // planes
        return jnp.exp(2.0 * (row.astype(F32) + 0.5) / total_rows)

    def y_flux(tile, width, q, u, v, w, p, c):
        reps = width // 128
        def rep(x):
            return x if reps == 1 else jnp.concatenate([x] * reps, axis=1)
        eta = (growth(tile, width) - 1.0) * (1.0 / DEN)
        kx, kz, kt = -eta * rep(slope_x), -eta * rep(slope_z), -eta * rep(rate)
        uc = kt + kx * u + v + kz * w
        nrm = 1.0 + eta * eta * rep(slope_sq)
        speed = jnp.abs(uc) + c * (nrm * lax.rsqrt(nrm))
        extra = {1: kx * p, 2: p, 3: kz * p, 4: p * (uc - kt)}
        for n in range(6):
            flux = q[n] * uc
            if n in extra:
                flux = flux + extra[n]
            for s, x in ((0, flux), (1, speed * q[n])):
                for lo, y in enumerate(split(x)):
                    slab = s + 2 * lo
                    for b in range(reps):
                        ys[tile + 1 + b, pl.ds(n * cols, cols), pl.ds(slab * 128, 128)] = (
                            y[:, b * 128 : (b + 1) * 128])

    for ref, tile in ((below, -1), (above, tiles)):
        gq = [ref[v] for v in range(6)]
        gr, gu, gv, gw, gp, gc = primitives(gq)
        y_flux(tile, 128, gq, gu, gv, gw, gp, gc)

    def phase_b(t, _):
        at = pl.ds(pl.multiple_of(t * wide, wide), wide)
        q = [q_ref[v, :, at] for v in range(6)]
        r, p, c = keep[0, :, at], keep[1, :, at], keep[2, :, at]
        y_flux(t * halves, wide, q, q[1] * r, q[2] * r, q[3] * r, p, c)
        return 0

    lax.fori_loop(0, length // wide, phase_b, 0)

    for m in mats[5:]:
        m.wait()

    inv_h = 1.0 / height
    scale = (-dt / 3.0) * inv_h
    decay = dt * rate * inv_h
    span = 4

    def dot(a, b):
        return jnp.dot(a, b, preferred_element_type=F32)

    def phase_c(gidx, _):
        t0 = gidx * span
        dx = dot(mx[...], rx[:, pl.ds(pl.multiple_of(t0 * 128, 128 * span), 128 * span)])
        dz = dot(zs[pl.ds(t0, span)].reshape(span * 6 * cols, 512), mz[...])
        dy = dot(ys[pl.ds(t0, span)].reshape(span * 6 * cols, 512), my[0])
        dy = dy + dot(ys[pl.ds(t0 + 1, span)].reshape(span * 6 * cols, 512), my[1])
        dy = dy + dot(ys[pl.ds(t0 + 2, span)].reshape(span * 6 * cols, 512), my[2])
        for b in range(span):
            at = pl.ds(pl.multiple_of((t0 + b) * 128, 128), 128)
            wy = (0.05 * total_rows * DEN / 2.0) / growth(t0 + b, 128)
            for v in range(6):
                lo = (b * 6 + v) * cols
                q = q_ref[v, :, at]
                d = dx[v * cols : (v + 1) * cols, b * 128 : (b + 1) * 128]
                d = d + dz[lo : lo + cols] + wy * dy[lo : lo + cols]
                new = q + scale * d - q * decay
                if v == 5:
                    new = new + dt * keep[3, :, at]
                out_ref[v, :, at] = new
        return 0

    lax.fori_loop(0, tiles // span, phase_c, 0)

    hl, hh = hx[5:8, :], hx[8 + cols : 11 + cols, :]
    heights = [jnp.concatenate([x] * groups, axis=0) for x in (hl, hh)]
    size = groups * 3

    def write(g, k):
        return pltpu.make_async_copy(
            out_ref.at[:, :, lanes(g, k)], out_hbm.at[:, :, lanes(g, k)], out_sem.at[k, g])

    for k in range(PARTS):
        @pl.when(has_l)
        def _(k=k):
            to_right(k).wait_recv()

        @pl.when(has_r)
        def _(k=k):
            to_left(k).wait_recv()

        for side, ref in enumerate((recv_lo, recv_hi)):
            q = [ref[k, v * size : (v + 1) * size, :] for v in range(6)]
            r, u, v, w, p, c = primitives(q)
            hv = heights[side] * u
            speed = jnp.abs(hv) + heights[side] * c
            for n in range(6):
                flux = hv * q[n]
                if n == 1:
                    flux = flux + heights[side] * p
                if n == 4:
                    flux = flux + hv * p
                fs, as_ = split(flux), split(speed * q[n])
                block = jnp.concatenate([fs[0].astype(F32), as_[0].astype(F32), fs[1].astype(F32), as_[1].astype(F32)], axis=0).astype(BF16)
                rh[side * 4 * size : (side + 1) * 4 * size, n * 128 : (n + 1) * 128] = block
        d = dot(mh[...], rh[...])
        for g in range(groups):
            for v in range(6):
                out_ref[v, :, lanes(g, k)] += scale * d[g * cols : (g + 1) * cols, v * 128 : (v + 1) * 128]
            write(g, k).start()

    for k in range(PARTS):
        for g in range(groups):
            write(g, k).wait()

    @pl.when(has_l)
    def _():
        h_left.wait_send()
        for k in range(PARTS):
            to_left(k).wait_send()

    @pl.when(has_r)
    def _():
        h_right.wait_send()
        for k in range(PARTS):
            to_right(k).wait_send()

    @pl.when(is_top)
    def _():
        for d in range(n_gy - 1):
            top_to(d).wait_send()

    @pl.when(has_b)
    def _():
        y_down.wait_send()

    @pl.when(has_a)
    def _():
        y_up.wait_send()


def finish(a_hbm, b_hbm, x_hbm, y_hbm, a, b, in_sem, out_sem):
    moves = [(a_hbm.at[v], a.at[v], x_hbm.at[v]) for v in range(6)] + [(b_hbm, b, y_hbm)]
    loads = [pltpu.make_async_copy(m[0], m[1], in_sem.at[i]) for i, m in enumerate(moves)]
    stores = [pltpu.make_async_copy(m[1], m[2], out_sem.at[i]) for i, m in enumerate(moves)]
    for c in loads:
        c.start()
    for c, d in zip(loads, stores):
        c.wait()
        d.start()
    for d in stores:
        d.wait()


def solution(mesh):
    n_gx, n_gy = mesh.shape["gx"], mesh.shape["gy"]

    def shards(state, shock_height, wall_segment, segment_level, blow_table):
        planes = blow_table.shape[1]
        cols, length = state.shape[1], state.shape[2]
        tiles = length // 128
        groups = tiles // PARTS
        mats = [jnp.asarray(m, BF16) for m in stencil_matrices(cols, planes)]
        vmem = pl.BlockSpec(memory_space=pltpu.VMEM)
        hbm = pl.BlockSpec(memory_space=pltpu.HBM)
        packed = pltpu.VMEM((PARTS, 18 * groups, 128), F32)
        tile6 = pltpu.VMEM((6, cols, 128), F32)
        sem = pltpu.SemaphoreType.DMA
        state_out, shock_out = pl.pallas_call(
            functools.partial(kernel, n_gx, n_gy, planes),
            out_shape=(
                jax.ShapeDtypeStruct(state.shape, F32),
                jax.ShapeDtypeStruct(shock_height.shape, F32),
            ),
            in_specs=[hbm] * 9,
            out_specs=(hbm, vmem),
            scratch_shapes=[
                pltpu.VMEM(state.shape, F32),
                pltpu.VMEM(state.shape, F32),
                pltpu.VMEM(shock_height.shape, F32),
                pltpu.SMEM(wall_segment.shape, jnp.int32),
                pltpu.SMEM(segment_level.shape, jnp.int32),
                pltpu.VMEM(blow_table.shape, F32),
                packed, packed, packed, packed,
                pltpu.VMEM((16 + cols, 128), F32),
                tile6, tile6, tile6,
                pltpu.VMEM((24 * cols, length), BF16),
                pltpu.VMEM((tiles, 6 * cols, 512), BF16),
                pltpu.VMEM((tiles + 2, 6 * cols, 512), BF16),
                pltpu.VMEM((4, cols, length), F32),
                pltpu.VMEM((24 * groups, 768), BF16),
                *[pltpu.VMEM(m.shape, BF16) for m in mats],
                pltpu.VMEM((cols, 128), F32),
                sem((9,)), sem((PARTS, groups)), sem((PARTS,)), sem((PARTS,)), sem((PARTS,)), sem((PARTS,)),
                sem((2,)), sem((2,)), sem((2,)), sem((2,)), sem((n_gy,)), sem,
            ],
            compiler_params=pltpu.CompilerParams(
                collective_id=0, has_side_effects=True, vmem_limit_bytes=62 * 1024 * 1024),
        )(state, shock_height, wall_segment, segment_level, blow_table, *mats)
        return pl.pallas_call(
            finish,
            out_shape=(
                jax.ShapeDtypeStruct(state.shape, F32),
                jax.ShapeDtypeStruct(shock_height.shape, F32),
            ),
            in_specs=[hbm, hbm],
            out_specs=(hbm, hbm),
            scratch_shapes=[
                pltpu.VMEM(state.shape, F32),
                pltpu.VMEM(shock_height.shape, F32),
                sem((7,)), sem((7,)),
            ],
            compiler_params=pltpu.CompilerParams(vmem_limit_bytes=62 * 1024 * 1024),
        )(state_out, shock_out)

    in_specs = (P(None, "gx", "gy"), P("gx", None), P("gx"), P(), P())
    out_specs = (P(None, "gx", "gy"), P("gx", None))
    return jax.shard_map(shards, mesh=mesh, in_specs=in_specs, out_specs=out_specs, check_vma=False)
```
